32 devices in a mesh: gx: 8 (over z, y), gz: 4 (over x, core).
Axes of the slice: x: 2, y: 2, z: 4, core: 2. Of those that a mesh axis runs over, the one named last changes fastest.
Arguments:
- populations: float32 [19, 32, 64, 128], P(None, 'gx', 'gz'), may hold values from 0.005 to 0.5, as said below
- relax_rates: float32 [19], replicated, may hold values from 0.6 to 1.9
- wall_flags: int32 [64, 128], replicated, may hold values 0 or 1
- particles: float32 [4, 8, 4, 2048], P(None, 'gx', 'gz'), may hold values from -2 to 2, as said below
- migrate_list: int32 [8, 4, 4, 128], P('gx', 'gz'), may hold values from -1 to 2047, as said below
- tile_slot: int32 [8, 4, 9, 1024], P('gx', 'gz'), may hold values from -1 to 2559, as said below
- tile_cell: int32 [8, 4, 9, 1024], P('gx', 'gz'), may hold values from 0 to 8191, as said below
- tile_weight: float32 [8, 4, 9, 1024], P('gx', 'gz'), may hold values from 0.1 to 1
Outputs:
- new_populations: float32 [19, 32, 64, 128], P(None, 'gx', 'gz')
The draws below stay inside these ranges and needn't reach their ends.
Inputs may be any that keep to these rules, and one draw needn't show every extreme that they name: `populations`: each is w_q (1 + 3 c_q.u + 0.25 e) for a node velocity u of small magnitude and e within -1 to 1, so every density lies near 1. `particles`: rows 0 to 2 are velocities, row 3 drag coefficients between 0.2 and 1. `migrate_list`: entry [i, k, d, m] is a slot of device (i, k) or -1; live entries come first in each list, and no slot appears twice among one device's four lists. List d sends to the next device along gx (d = 0), the previous along gx (1), the next along gz (2), the previous along gz (3). A list may be full. `tile_slot`: entry [i, k, j, m] is a slot of that device's resident particles or -1; live entries come first in each bucket, and a bucket may be full. `tile_cell`: bucket j addresses the device j // 3 - 1 steps along gx and j % 3 - 1 along gz; a tile for a device one step along an axis lies in that device's plane of nodes facing the sender along that axis.
All inputs are finite; a program needn't handle non-finite values.
Results may differ from the reference program's by a relative error of at most 0.0003.
Values sent between devices are 32-bit elements; how exact they have to be, the bound alone decides.
A program may use at most 64 MiB of HBM per device.

```python
import math
import jax
import jax.numpy as jnp
import numpy as np
from jax import lax

CX = 4
CZ = 16
NY = 128
P_DEV = 2048
MIG = 128
CAP = 1024
P_ALL = 2560
NX = 32
NZ = 64
N_GX = 8
N_GZ = 4


def lattice_velocities_drawn():
    return np.array([[0, 0, 0], [1, 0, 0], [-1, 0, 0], [0, 1, 0], [0, -1, 0], [0, 0, 1], [0, 0, -1], [1, 1, 0], [-1, -1, 0], [1, -1, 0], [-1, 1, 0], [1, 0, 1], [-1, 0, -1], [1, 0, -1], [-1, 0, 1], [0, 1, 1], [0, -1, -1], [0, 1, -1], [0, -1, 1]]) * 1.0


def lattice_weights_drawn():
    return np.array([1.0 / 3.0] + [1.0 / 18.0] * 6 + [1.0 / 36.0] * 12)


def draw_populations(key, part):
    table = lattice_velocities_drawn()
    weights = jnp.asarray(lattice_weights_drawn(), jnp.float32).reshape(19, 1, 1, 1)
    first, second = jax.random.split(jax.random.fold_in(key, 3))
    flow = jax.random.uniform(first, (3, NX, NZ, NY), jnp.float32, -0.05, 0.05)
    noise = jax.random.uniform(second, (19, NX, NZ, NY), jnp.float32, -1.0, 1.0)
    along = jnp.stack([float(table[direction, 0]) * flow[0] + float(table[direction, 1]) * flow[1] + float(table[direction, 2]) * flow[2] for direction in range(19)])
    return weights * (1.0 + 3.0 * along + 0.25 * noise)


def draw_particles(key, part):
    first, second = jax.random.split(jax.random.fold_in(key, 5))
    speeds = 0.5 * jnp.clip(jax.random.normal(first, (3, N_GX, N_GZ, P_DEV), jnp.float32), -4.0, 4.0)
    drag = jnp.exp(jax.random.uniform(second, (1, N_GX, N_GZ, P_DEV), jnp.float32, math.log(0.2), 0.0))
    return jnp.concatenate([speeds, drag], axis=0)


def slab_levels(key):
    levels = jax.random.randint(jax.random.fold_in(key, 7), (N_GX,), 1, 5)
    return jnp.where(levels == jnp.max(levels), 4, levels).astype(jnp.int32)


def draw_migrate_list(key, part):
    levels = slab_levels(key)[:, None, None]
    order_keys = jax.random.split(jax.random.fold_in(key, 11), N_GX * N_GZ)
    orders = jax.vmap(lambda single: jax.random.permutation(single, P_DEV)[:4 * MIG])(order_keys)
    orders = orders.reshape(N_GX, N_GZ, 4, MIG).astype(jnp.int32)
    jitter = jax.random.randint(jax.random.fold_in(key, 13), (N_GX, N_GZ, 4), 0, MIG // 8 + 1)
    counts = jnp.where(levels == 4, MIG, jnp.maximum(levels * levels * MIG // 16 - jitter, 0))
    position = jnp.arange(MIG, dtype=jnp.int32)
    return jnp.where(position < counts[..., None], orders, -1).astype(jnp.int32)


def draw_tile_slot(key, part):
    levels = slab_levels(key)[:, None, None]
    bucket = jnp.arange(9, dtype=jnp.int32)[None, None, :]
    jitter = jax.random.randint(jax.random.fold_in(key, 17), (N_GX, N_GZ, 9), 0, CAP // 8 + 1)
    counts = jnp.where((levels == 4) | (bucket == 4), CAP, jnp.maximum(levels * levels * CAP // 16 - jitter, 0))
    slots = jax.random.randint(jax.random.fold_in(key, 19), (N_GX, N_GZ, 9, CAP), 0, P_ALL)
    position = jnp.arange(CAP, dtype=jnp.int32)
    return jnp.where(position < counts[..., None], slots, -1).astype(jnp.int32)


def draw_tile_cell(key, part):
    bucket = jnp.arange(9, dtype=jnp.int32)
    step_x = (bucket // 3 - 1)[None, None, :, None]
    step_z = (bucket % 3 - 1)[None, None, :, None]
    shape = (N_GX, N_GZ, 9, CAP)
    local_x = jax.random.randint(jax.random.fold_in(key, 23), shape, 0, CX)
    local_z = jax.random.randint(jax.random.fold_in(key, 29), shape, 0, CZ)
    local_y = jax.random.randint(jax.random.fold_in(key, 31), shape, 0, NY)
    local_x = jnp.where(step_x == 1, 0, jnp.where(step_x == -1, CX - 1, local_x))
    local_z = jnp.where(step_z == 1, 0, jnp.where(step_z == -1, CZ - 1, local_z))
    return ((local_x * CZ + local_z) * NY + local_y).astype(jnp.int32)


def set_ends(entries, key, least, largest):
    place = [jax.random.randint(jax.random.fold_in(key, axis), (), 0, length) for axis, length in enumerate(entries.shape)]
    widest = entries.shape.index(max(entries.shape))
    beside = place[:widest] + [(place[widest] + 1) % entries.shape[widest]] + place[widest + 1:]
    return entries.at[tuple(place)].set(least).at[tuple(beside)].set(largest)


def shard_levels(own_key, shape, cuts, low, high):
    level, own = 1.0, jax.random.fold_in(own_key, 6)
    for axis_at, parts in cuts:
        heights = jnp.exp(jax.random.uniform(jax.random.fold_in(own, axis_at), (parts,), jnp.float32, low / len(cuts), high / len(cuts)))
        level = level * jnp.repeat(heights, shape[axis_at] // parts).reshape([-1 if axis == axis_at else 1 for axis in range(len(shape))])
    return level


def setup_inputs(seed: int = 0) -> dict:
    key_of = jax.random.split(jax.random.key(seed), 9)
    populations = draw_populations(jax.random.fold_in(key_of[8], 71), 0)
    relax_rates = jnp.clip(jnp.exp(jax.random.uniform(key_of[1], (19,), jnp.float32, math.log(0.6), math.log(1.9))), 0.6, 1.9)
    wall_flags = set_ends((jax.random.randint(key_of[2], (NZ, NY), 0, 16) < 1).astype(jnp.int32), jax.random.fold_in(key_of[2], 1), 0, 1)
    particles = draw_particles(jax.random.fold_in(key_of[8], 71), 0)
    migrate_list = draw_migrate_list(jax.random.fold_in(key_of[8], 71), 0)
    tile_slot = draw_tile_slot(jax.random.fold_in(key_of[8], 71), 0)
    tile_cell = draw_tile_cell(jax.random.fold_in(key_of[8], 71), 0)
    tile_weight = jnp.clip(jnp.exp(math.log(1.0) - 2.3025851 * jax.random.uniform(key_of[7], (N_GX, N_GZ, 9, CAP), jnp.float32) ** shard_levels(key_of[7], (N_GX, N_GZ, 9, CAP), ((0, 8), (1, 4)), -0.2, 0.2)), 0.1, 1.0)
    return dict(populations=populations, relax_rates=relax_rates, wall_flags=wall_flags, particles=particles, migrate_list=migrate_list, tile_slot=tile_slot, tile_cell=tile_cell, tile_weight=tile_weight)


def lattice_velocities():
    return np.array([[0, 0, 0], [1, 0, 0], [-1, 0, 0], [0, 1, 0], [0, -1, 0], [0, 0, 1], [0, 0, -1], [1, 1, 0], [-1, -1, 0], [1, -1, 0], [-1, 1, 0], [1, 0, 1], [-1, 0, -1], [1, 0, -1], [-1, 0, 1], [0, 1, 1], [0, -1, -1], [0, 1, -1], [0, -1, 1]]) * 1.0

def lattice_weights():
    return np.array([1.0 / 3.0] + [1.0 / 18.0] * 6 + [1.0 / 36.0] * 12)

def opposite_table():
    table = lattice_velocities()
    return [int(np.argmax(np.all(table == -entry, axis=1))) for entry in table]

def moment_basis():
    table = lattice_velocities()
    along_x, along_y, along_z = (table[:, 0], table[:, 1], table[:, 2])
    square = along_x * along_x + along_y * along_y + along_z * along_z
    raw_list = [np.ones(19), square, square * square, along_x, along_y, along_z, square * along_x, square * along_y, square * along_z, 3 * along_x * along_x - square, square * (3 * along_x * along_x - square), along_y * along_y - along_z * along_z, square * (along_y * along_y - along_z * along_z), along_x * along_y, along_y * along_z, along_x * along_z, along_x * (along_y * along_y - along_z * along_z), along_y * (along_z * along_z - along_x * along_x), along_z * (along_x * along_x - along_y * along_y)]
    basis = []
    for vector in raw_list:
        vector = np.array(vector) * 1.0
        for earlier in basis:
            vector = vector - np.dot(vector, earlier) * earlier
        basis.append(vector / np.sqrt(np.dot(vector, vector)))
    return np.stack(basis)

def collision_operator(relax_rates):
    basis = jnp.asarray(moment_basis(), jnp.float32)
    keep_mask = jnp.asarray(np.array([0, 1, 1, 0, 0, 0] + [1] * 13) * 1.0, jnp.float32)
    scaled = relax_rates * keep_mask
    return jnp.dot(basis.T * scaled[None, :], basis, precision=lax.Precision.HIGHEST)

def collide(populations, force_sums, relax_rates):
    highest = lax.Precision.HIGHEST
    velocities = jnp.asarray(lattice_velocities(), jnp.float32)
    weights = jnp.asarray(lattice_weights(), jnp.float32).reshape(19, 1, 1, 1)
    density = lax.optimization_barrier(jnp.sum(populations, axis=0))
    momentum = jnp.tensordot(velocities.T, populations, axes=1, precision=highest)
    force = force_sums[:3] - force_sums[3] * (momentum / density)
    velocity = (momentum + 0.5 * force) / density
    along_u = jnp.tensordot(velocities, velocity, axes=1, precision=highest)
    along_f = jnp.tensordot(velocities, force, axes=1, precision=highest)
    speed_sq = lax.optimization_barrier(jnp.sum(velocity * velocity, axis=0))
    u_dot_f = lax.optimization_barrier(jnp.sum(velocity * force, axis=0))
    equilibrium = weights * density * (1.0 + 3.0 * along_u + 4.5 * along_u * along_u - 1.5 * speed_sq)
    source = weights * (3.0 * along_f - 3.0 * u_dot_f + 9.0 * along_u * along_f)
    departure = populations - equilibrium + 0.5 * source
    relaxed = jnp.tensordot(collision_operator(relax_rates), departure, axes=1, precision=highest)
    return populations + source - relaxed

def shift_wall(field, offset, fill):
    if offset == 0:
        return field
    border = jnp.full_like(field[..., :1], fill)
    if offset == 1:
        return jnp.concatenate([border, field[..., :-1]], axis=-1)
    return jnp.concatenate([field[..., 1:], border], axis=-1)

def solid_nodes(wall_flags):
    depth_y = wall_flags.shape[1]
    height = lax.broadcasted_iota(jnp.int32, wall_flags.shape, 1)
    boundary = (height == 0) | (height == depth_y - 1)
    return jnp.where(boundary, 1, wall_flags).astype(jnp.int32)

def pick_columns(table, index):
    taken = jnp.take(table, jnp.maximum(index, 0), axis=1)
    return jnp.where(index >= 0, taken, 0.0)

def depart(own_slots, lists):
    leaving = jnp.stack([pick_columns(own_slots, lists[target]) for target in range(4)])
    flat_list = lists.reshape(-1)
    gone = jnp.zeros((own_slots.shape[1],), jnp.float32).at[jnp.maximum(flat_list, 0)].max((flat_list >= 0).astype(jnp.float32))
    return (own_slots * (1.0 - gone)[None, :], leaving)

def tile_values(resident, slots, weights):
    picked = pick_columns(resident, slots)
    scale = weights * picked[3]
    return jnp.stack([scale * picked[0], scale * picked[1], scale * picked[2], scale])

def stream_global(collided, solid):
    table = lattice_velocities()
    opposite = opposite_table()
    outputs = []
    for direction in range(19):
        step_x, step_y, step_z = [int(entry) for entry in table[direction]]
        moved = jnp.roll(collided[direction], (step_x, step_z), axis=(0, 1))
        moved = shift_wall(moved, step_y, 0.0)
        blocked = shift_wall(jnp.roll(solid, step_z, axis=0), step_y, 1)
        outputs.append(jnp.where(blocked[None] > 0, collided[opposite[direction]], moved))
    return jnp.stack(outputs)

def reference(populations, relax_rates, wall_flags, particles, migrate_list, tile_slot, tile_cell, tile_weight):
    per_device = jnp.moveaxis(particles, 0, 2)
    staying, leaving = jax.vmap(jax.vmap(depart))(per_device, migrate_list)
    arrivals = [jnp.roll(leaving[:, :, 0], 1, axis=0), jnp.roll(leaving[:, :, 1], -1, axis=0), jnp.roll(leaving[:, :, 2], 1, axis=1), jnp.roll(leaving[:, :, 3], -1, axis=1)]
    resident = jnp.concatenate([staying] + arrivals, axis=3)
    values = jax.vmap(jax.vmap(tile_values))(resident, tile_slot, tile_weight)
    slab_x = jnp.arange(N_GX, dtype=jnp.int32)[:, None, None, None]
    slab_z = jnp.arange(N_GZ, dtype=jnp.int32)[None, :, None, None]
    bucket = jnp.arange(9, dtype=jnp.int32)[None, None, :, None]
    owner_x = (slab_x + bucket // 3 - 1) % N_GX
    owner_z = (slab_z + bucket % 3 - 1) % N_GZ
    local_x = tile_cell // (CZ * NY)
    local_z = tile_cell // NY % CZ
    local_y = tile_cell % NY
    target = ((owner_x * CX + local_x) * NZ + owner_z * CZ + local_z) * NY + local_y
    flat_values = jnp.moveaxis(values, 2, 0).reshape(4, -1)
    force_sums = jnp.zeros((4, NX * NZ * NY), jnp.float32).at[:, target.reshape(-1)].add(flat_values)
    force_sums = force_sums.reshape(4, NX, NZ, NY)
    collided = collide(populations, force_sums, relax_rates)
    return stream_global(collided, solid_nodes(wall_flags))
```

```python
import jax
import jax.numpy as jnp
import numpy as np
from jax import lax
from jax.experimental import pallas as pl
from jax.experimental.pallas import tpu as pltpu
from jax.sharding import PartitionSpec as P

MESH = pl.DeviceIdType.MESH
VELOCITIES = [
    (0, 0, 0),
    (1, 0, 0),
    (-1, 0, 0),
    (0, 1, 0),
    (0, -1, 0),
    (0, 0, 1),
    (0, 0, -1),
    (1, 1, 0),
    (-1, -1, 0),
    (1, -1, 0),
    (-1, 1, 0),
    (1, 0, 1),
    (-1, 0, -1),
    (1, 0, -1),
    (-1, 0, 1),
    (0, 1, 1),
    (0, -1, -1),
    (0, 1, -1),
    (0, -1, 1),
]
WEIGHTS = [1.0 / 3.0] + [1.0 / 18.0] * 6 + [1.0 / 36.0] * 12
OPPOSITE = [VELOCITIES.index((-a, -b, -c)) for a, b, c in VELOCITIES]
PAIRS = [(q, OPPOSITE[q]) for q in range(1, 19) if q < OPPOSITE[q]]
ALONG_X = [[q for q in range(19) if VELOCITIES[q][0] == s] for s in (1, -1)]
ALONG_Z = [[q for q in range(19) if VELOCITIES[q][2] == s] for s in (1, -1)]
STEP = (1, -1)
CORNERS = [(0, 0), (0, 1), (1, 0), (1, 1)]
PAD = 8


def moment_basis():
    table = np.array(VELOCITIES) * 1.0
    x, y, z = table[:, 0], table[:, 1], table[:, 2]
    square = x * x + y * y + z * z
    raw_list = [
        np.ones(19),
        square,
        square * square,
        x,
        y,
        z,
        square * x,
        square * y,
        square * z,
        3 * x * x - square,
        square * (3 * x * x - square),
        y * y - z * z,
        square * (y * y - z * z),
        x * y,
        y * z,
        x * z,
        x * (y * y - z * z),
        y * (z * z - x * x),
        z * (x * x - y * y),
    ]
    basis = []
    for vector in raw_list:
        for earlier in basis:
            vector = vector - np.dot(vector, earlier) * earlier
        basis.append(vector / np.sqrt(np.dot(vector, vector)))
    return np.stack(basis)


BASIS = moment_basis()
EVEN = [1, 2, 9, 10, 11, 12, 13, 14, 15]
ODD = [6, 7, 8, 16, 17, 18]


def combine(coefficients, values):
    groups = {}
    for coefficient, value in zip(coefficients, values):
        if abs(coefficient) < 1e-9:
            continue
        groups.setdefault(round(abs(coefficient), 9), []).append((float(coefficient), value))
    total = None
    for members in groups.values():
        size = abs(members[0][0])
        lead = 1.0 if members[0][0] > 0 else -1.0
        part = members[0][1]
        for coefficient, value in members[1:]:
            part = part + value if coefficient * lead > 0 else part - value
        if total is None:
            total = part * (size * lead)
        else:
            total = total + part * (size * lead)
    return total


def collide(pops, forces, rates, wanted):
    sums = [pops[a] + pops[b] for a, b in PAIRS]
    gaps = [pops[a] - pops[b] for a, b in PAIRS]
    density = pops[0]
    for entry in sums:
        density = density + entry
    momentum = [
        combine([VELOCITIES[a][axis] for a, _ in PAIRS], gaps) for axis in range(3)
    ]
    inverse = 1.0 / density
    force = [forces[axis] - forces[3] * (momentum[axis] * inverse) for axis in range(3)]
    velocity = [(momentum[axis] + 0.5 * force[axis]) * inverse for axis in range(3)]
    speed_sq = velocity[0] * velocity[0] + velocity[1] * velocity[1] + velocity[2] * velocity[2]
    u_dot_f = velocity[0] * force[0] + velocity[1] * force[1] + velocity[2] * force[2]
    base = 1.0 - 1.5 * speed_sq
    density_odd = 6.0 * density
    rest_source = (-3.0 * WEIGHTS[0]) * u_dot_f
    rest = pops[0] - WEIGHTS[0] * (density * base) + 0.5 * rest_source
    even_in, odd_in, even_source, odd_source = [rest], [], [], []
    for index, (a, _) in enumerate(PAIRS):
        along_u = combine(VELOCITIES[a], velocity)
        along_f = combine(VELOCITIES[a], force)
        weight = WEIGHTS[a]
        source_even = weight * (9.0 * along_u * along_f - 3.0 * u_dot_f)
        source_odd = (3.0 * weight) * along_f
        even_in.append(
            sums[index]
            - (2.0 * weight) * (density * (base + 4.5 * along_u * along_u))
            + source_even
        )
        odd_in.append(gaps[index] - weight * (density_odd * along_u) + source_odd)
        even_source.append(source_even)
        odd_source.append(source_odd)
    firsts = [a for a, _ in PAIRS]
    even_m = [rates[k] * combine(BASIS[k][[0] + firsts], even_in) for k in EVEN]
    odd_m = [rates[k] * combine(BASIS[k][firsts], odd_in) for k in ODD]
    out = {}
    if 0 in wanted:
        out[0] = pops[0] + rest_source - combine(BASIS[EVEN, 0], even_m)
    for index, (a, b) in enumerate(PAIRS):
        if a not in wanted and b not in wanted:
            continue
        even = even_source[index] - combine(BASIS[EVEN, a], even_m)
        odd = odd_source[index] - combine(BASIS[ODD, a], odd_m)
        out[a] = pops[a] + even + odd
        out[b] = pops[b] + even - odd
    return out


def lane_pick(row, lanes):
    table = jnp.broadcast_to(row, lanes.shape)
    return jnp.take_along_axis(table, lanes, axis=1, mode="promise_in_bounds")


def spread(values, rows, lanes, count):
    highs = [v.astype(jnp.bfloat16).astype(jnp.float32) for v in values]
    parts = highs + [v - h for v, h in zip(values, highs)]
    row_iota = lax.broadcasted_iota(jnp.int32, (count, 128), 0)
    lane_iota = lax.broadcasted_iota(jnp.int32, (128, 128), 0)
    left, right = [], []
    for s in range(8):
        hit = row_iota == rows[s : s + 1]
        left.append(
            jnp.concatenate(
                [jnp.where(hit, part[s : s + 1], 0.0) for part in parts], axis=0
            ).astype(jnp.bfloat16)
        )
        right.append(jnp.where(lane_iota == lanes[s : s + 1], 1.0, 0.0).astype(jnp.bfloat16))
    both = lax.dot_general(
        jnp.concatenate(left, axis=1),
        jnp.concatenate(right, axis=1),
        (((1,), (1,)), ((), ())),
        preferred_element_type=jnp.float32,
    )
    return both[: 4 * count] + both[4 * count :]


def kernel(
    devices_x,
    devices_z,
    pops_ref,
    rates_ref,
    wall_ref,
    part_ref,
    list_ref,
    slot_ref,
    cell_ref,
    weight_ref,
    out_ref,
    stay,
    leave,
    arrive,
    values,
    force,
    plane_out,
    plane_in,
    edge_out,
    edge_in,
    corner_in,
    coll,
    halo_x_out,
    halo_x_in,
    halo_z_out,
    halo_z_in,
    halo_c_in,
    solid,
    send_sem,
    recv_sem,
):
    me_x, me_z = lax.axis_index("gx"), lax.axis_index("gz")
    depth_z = 16
    rows_z = wall_ref.shape[0]

    def peer(step_x, step_z):
        return (
            lax.rem(me_x + step_x + devices_x, devices_x),
            lax.rem(me_z + step_z + devices_z, devices_z),
        )

    barrier = pltpu.get_barrier_semaphore()
    around = [(a, b) for a in (-1, 0, 1) for b in (-1, 0, 1) if (a, b) != (0, 0)]
    for step in around:
        pl.semaphore_signal(barrier, inc=1, device_id=peer(*step), device_id_type=MESH)

    count = [0]

    def send(source, target, step):
        at = count[0]
        count[0] += 1
        copy = pltpu.make_async_remote_copy(
            src_ref=source,
            dst_ref=target,
            send_sem=send_sem.at[at],
            recv_sem=recv_sem.at[at],
            device_id=peer(*step),
            device_id_type=MESH,
        )
        copy.start()
        return copy

    lists = list_ref[...]
    lists8 = jnp.concatenate([lists, lists], axis=0)
    list_hi, list_lo = lists8 >> 7, lists8 & 127
    picked = [jnp.zeros((8, 128), jnp.float32) for _ in range(4)]
    for h in range(16):
        hit = list_hi == h
        for c in range(4):
            picked[c] = jnp.where(
                hit, lane_pick(part_ref[c * 16 + h : c * 16 + h + 1], list_lo), picked[c]
            )
    for c in range(4):
        for d in range(4):
            leave[d, c : c + 1, :] = picked[c][d : d + 1]
    pl.semaphore_wait(barrier, len(around))
    migrations = [
        send(leave.at[d], arrive.at[d], step)
        for d, step in enumerate([(1, 0), (-1, 0), (0, 1), (0, -1)])
    ]

    hi_iota = lax.broadcasted_iota(jnp.int32, (16, 128), 0)
    lo_iota = lax.broadcasted_iota(jnp.int32, (128, 128), 0)
    left = jnp.concatenate(
        [jnp.where(hi_iota == list_hi[d : d + 1], 1.0, 0.0) for d in range(4)], axis=1
    ).astype(jnp.bfloat16)
    right = jnp.concatenate(
        [jnp.where(lo_iota == list_lo[d : d + 1], 1.0, 0.0) for d in range(4)], axis=1
    ).astype(jnp.bfloat16)
    gone = lax.dot_general(
        left, right, (((1,), (1,)), ((), ())), preferred_element_type=jnp.float32
    )
    for c in range(4):
        stay[c] = jnp.where(gone > 0.5, 0.0, part_ref[c * 16 : c * 16 + 16])

    def first_pick(j, carry):
        at = pl.ds(pl.multiple_of(j * 8, 8), 8)
        slots = slot_ref[at]
        hi, lo = slots >> 7, slots & 127
        got = [jnp.zeros((8, 128), jnp.float32) for _ in range(4)]
        for h in range(16):
            hit = hi == h
            for c in range(4):
                got[c] = jnp.where(hit, lane_pick(stay[c, h : h + 1], lo), got[c])
        for c in range(4):
            values[c, at] = got[c]
        return carry

    lax.fori_loop(0, 9, first_pick, 0)

    wall = jnp.where(
        (lax.broadcasted_iota(jnp.int32, (depth_z, 128), 1) == 0)
        | (lax.broadcasted_iota(jnp.int32, (depth_z, 128), 1) == 127),
        1,
        wall_ref[pl.ds(pl.multiple_of(me_z * depth_z, depth_z), depth_z)],
    )
    solid[PAD : PAD + depth_z] = wall
    lane = lax.broadcasted_iota(jnp.int32, (1, 128), 1)
    ends = (lane == 0) | (lane == 127)
    below = lax.rem(me_z * depth_z + rows_z - 1, rows_z)
    above = lax.rem(me_z * depth_z + depth_z, rows_z)
    solid[PAD - 1 : PAD] = jnp.where(ends, 1, wall_ref[pl.ds(below, 1)])
    solid[PAD + depth_z : PAD + depth_z + 1] = jnp.where(ends, 1, wall_ref[pl.ds(above, 1)])

    for copy in migrations:
        copy.wait()

    def second_pick(j, carry):
        at = pl.ds(pl.multiple_of(j * 8, 8), 8)
        slots = slot_ref[at]
        hi, lo = slots >> 7, slots & 127
        got = [values[c, at] for c in range(4)]
        for d in range(4):
            hit = hi == 16 + d
            for c in range(4):
                got[c] = jnp.where(hit, lane_pick(arrive[d, c : c + 1], lo), got[c])
        scale = weight_ref[at] * got[3]
        for c in range(3):
            values[c, at] = scale * got[c]
        values[3, at] = scale
        return carry

    lax.fori_loop(0, 9, second_pick, 0)

    def bucket(step_x, step_z):
        at = ((step_x + 1) * 3 + step_z + 1) * 8
        cells = cell_ref[at : at + 8]
        return [values[c, at : at + 8] for c in range(4)], cells

    exchanges = []
    for s, step in enumerate(STEP):
        got, cells = bucket(step, 0)
        plane_out[s] = spread(got, (cells >> 7) & 15, cells & 127, 16).reshape(4, 16, 128)
        exchanges.append(send(plane_out.at[s], plane_in.at[s], (step, 0)))
    for s, step in enumerate(STEP):
        total = None
        for step_x in (-1, 0, 1):
            got, cells = bucket(step_x, step)
            rows = (cells >> 11) + 1 if step_x == 0 else jnp.full_like(cells, 0 if step_x < 0 else 5)
            part = spread(got, rows, cells & 127, 8)
            total = part if total is None else total + part
        edge_out[s] = total.reshape(4, 8, 128)
        exchanges.append(send(edge_out.at[s], edge_in.at[s], (0, step)))
        for sx, step_x in enumerate(STEP):
            exchanges.append(send(edge_out.at[s], corner_in.at[s * 2 + sx], (step_x, step)))
    got, cells = bucket(0, 0)
    force[...] = spread(got, cells >> 7, cells & 127, 64).reshape(4, 4, 16, 128)
    for copy in exchanges:
        copy.wait()
    for s in range(2):
        x = 0 if s == 0 else 3
        for c in range(4):
            force[c, x] = force[c, x] + plane_in[s, c]
    for s in range(2):
        z = 0 if s == 0 else 15
        for c in range(4):
            for x in range(4):
                row = edge_in[s, c, x + 1 : x + 2]
                if x == 0:
                    row = row + corner_in[s * 2, c, 5:6]
                if x == 3:
                    row = row + corner_in[s * 2 + 1, c, 0:1]
                force[c, x, z : z + 1] = force[c, x, z : z + 1] + row

    rates = [rates_ref[k] for k in range(19)]
    halos = []
    for x in (3, 0, 1, 2):
        done = collide(
            [pops_ref[q, x] for q in range(19)],
            [force[c, x] for c in range(4)],
            rates,
            range(19),
        )
        for q in range(19):
            coll[q, 1 + x, PAD : PAD + 16] = done[q]
        for s in range(2):
            z = 15 if s == 0 else 0
            for n, q in enumerate(ALONG_Z[s]):
                halo_z_out[s, n, x : x + 1] = done[q][z : z + 1]
        if x in (3, 0):
            s = 0 if x == 3 else 1
            for n, q in enumerate(ALONG_X[s]):
                halo_x_out[s, n] = done[q]
            halos.append(send(halo_x_out.at[s], halo_x_in.at[s], (STEP[s], 0)))
    for s in range(2):
        halos.append(send(halo_z_out.at[s], halo_z_in.at[s], (0, STEP[s])))
        for sx in range(2):
            q = VELOCITIES.index((STEP[sx], 0, STEP[s]))
            n = ALONG_Z[s].index(q)
            halos.append(
                send(halo_z_out.at[s, n], halo_c_in.at[s * 2 + sx], (STEP[sx], STEP[s]))
            )
    for copy in halos:
        copy.wait()
    for s in range(2):
        for n, q in enumerate(ALONG_X[s]):
            coll[q, 0 if s == 0 else 5, PAD : PAD + 16] = halo_x_in[s, n]
        z = PAD - 1 if s == 0 else PAD + 16
        for n, q in enumerate(ALONG_Z[s]):
            for x in range(4):
                coll[q, 1 + x, z : z + 1] = halo_z_in[s, n, x : x + 1]
        for sx in range(2):
            q = VELOCITIES.index((STEP[sx], 0, STEP[s]))
            x = 3 if sx == 0 else 0
            coll[q, 0 if sx == 0 else 5, z : z + 1] = halo_c_in[s * 2 + sx, x : x + 1]

    for q in range(19):
        step_x, step_y, step_z = VELOCITIES[q]
        blocked = solid[PAD - step_z : PAD - step_z + 16]
        if step_y:
            blocked = pltpu.roll(blocked, step_y % 128, 1)
        for x in range(4):
            moved = coll[q, 1 + x - step_x, PAD - step_z : PAD - step_z + 16]
            if step_y:
                moved = pltpu.roll(moved, step_y % 128, 1)
            out_ref[q, x] = jnp.where(
                blocked > 0, coll[OPPOSITE[q], 1 + x, PAD : PAD + 16], moved
            )


def solution(mesh):
    devices_x, devices_z = mesh.shape["gx"], mesh.shape["gz"]

    def body(pops, rates, wall, particles, lists, slot, cell, weight):
        vmem = pl.BlockSpec(memory_space=pltpu.VMEM)
        smem = pl.BlockSpec(memory_space=pltpu.SMEM)
        f32 = jnp.float32
        return pl.pallas_call(
            lambda *refs: kernel(devices_x, devices_z, *refs),
            out_shape=jax.ShapeDtypeStruct(pops.shape, f32),
            in_specs=[vmem, smem] + [vmem] * 6,
            out_specs=vmem,
            scratch_shapes=[
                pltpu.VMEM((4, 16, 128), f32),
                pltpu.VMEM((4, 8, 128), f32),
                pltpu.VMEM((4, 8, 128), f32),
                pltpu.VMEM((4, 72, 128), f32),
                pltpu.VMEM((4, 4, 16, 128), f32),
                pltpu.VMEM((2, 4, 16, 128), f32),
                pltpu.VMEM((2, 4, 16, 128), f32),
                pltpu.VMEM((2, 4, 8, 128), f32),
                pltpu.VMEM((2, 4, 8, 128), f32),
                pltpu.VMEM((4, 4, 8, 128), f32),
                pltpu.VMEM((19, 6, 32, 128), f32),
                pltpu.VMEM((2, 5, 16, 128), f32),
                pltpu.VMEM((2, 5, 16, 128), f32),
                pltpu.VMEM((2, 5, 8, 128), f32),
                pltpu.VMEM((2, 5, 8, 128), f32),
                pltpu.VMEM((4, 8, 128), f32),
                pltpu.VMEM((32, 128), jnp.int32),
                pltpu.SemaphoreType.DMA((20,)),
                pltpu.SemaphoreType.DMA((20,)),
            ],
            compiler_params=pltpu.CompilerParams(
                collective_id=0, has_side_effects=True, vmem_limit_bytes=48 * 1024 * 1024
            ),
        )(
            pops,
            rates,
            wall,
            particles.reshape(64, 128),
            lists.reshape(4, 128),
            slot.reshape(72, 128),
            cell.reshape(72, 128),
            weight.reshape(72, 128),
        )

    return jax.shard_map(
        body,
        mesh=mesh,
        in_specs=(
            P(None, "gx", "gz", None),
            P(),
            P(),
            P(None, "gx", "gz", None),
            P("gx", "gz", None, None),
            P("gx", "gz", None, None),
            P("gx", "gz", None, None),
            P("gx", "gz", None, None),
        ),
        out_specs=P(None, "gx", "gz", None),
        check_vma=False,
    )
```

```python
import jax
import jax.numpy as jnp
import numpy as np
from jax import lax
from jax.experimental import pallas as pl
from jax.experimental.pallas import tpu as pltpu
from jax.sharding import PartitionSpec as P

MESH = pl.DeviceIdType.MESH
VELOCITIES = [
    (0, 0, 0),
    (1, 0, 0),
    (-1, 0, 0),
    (0, 1, 0),
    (0, -1, 0),
    (0, 0, 1),
    (0, 0, -1),
    (1, 1, 0),
    (-1, -1, 0),
    (1, -1, 0),
    (-1, 1, 0),
    (1, 0, 1),
    (-1, 0, -1),
    (1, 0, -1),
    (-1, 0, 1),
    (0, 1, 1),
    (0, -1, -1),
    (0, 1, -1),
    (0, -1, 1),
]
WEIGHTS = [1.0 / 3.0] + [1.0 / 18.0] * 6 + [1.0 / 36.0] * 12
OPPOSITE = [VELOCITIES.index((-a, -b, -c)) for a, b, c in VELOCITIES]
PAIRS = [(q, OPPOSITE[q]) for q in range(1, 19) if q < OPPOSITE[q]]
ALONG_X = [[q for q in range(19) if VELOCITIES[q][0] == s] for s in (1, -1)]
ALONG_Z = [[q for q in range(19) if VELOCITIES[q][2] == s] for s in (1, -1)]
STEP = (1, -1)
CORNERS = [(0, 0), (0, 1), (1, 0), (1, 1)]
PAD = 8


def moment_basis():
    table = np.array(VELOCITIES) * 1.0
    x, y, z = table[:, 0], table[:, 1], table[:, 2]
    square = x * x + y * y + z * z
    raw_list = [
        np.ones(19),
        square,
        square * square,
        x,
        y,
        z,
        square * x,
        square * y,
        square * z,
        3 * x * x - square,
        square * (3 * x * x - square),
        y * y - z * z,
        square * (y * y - z * z),
        x * y,
        y * z,
        x * z,
        x * (y * y - z * z),
        y * (z * z - x * x),
        z * (x * x - y * y),
    ]
    basis = []
    for vector in raw_list:
        for earlier in basis:
            vector = vector - np.dot(vector, earlier) * earlier
        basis.append(vector / np.sqrt(np.dot(vector, vector)))
    return np.stack(basis)


BASIS = moment_basis()
EVEN = [1, 2, 9, 10, 11, 12, 13, 14, 15]
ODD = [6, 7, 8, 16, 17, 18]


def combine(coefficients, values):
    groups = {}
    for coefficient, value in zip(coefficients, values):
        if abs(coefficient) < 1e-9:
            continue
        groups.setdefault(round(abs(coefficient), 9), []).append((float(coefficient), value))
    total = None
    for members in groups.values():
        size = abs(members[0][0])
        lead = 1.0 if members[0][0] > 0 else -1.0
        part = members[0][1]
        for coefficient, value in members[1:]:
            part = part + value if coefficient * lead > 0 else part - value
        if total is None:
            total = part * (size * lead)
        else:
            total = total + part * (size * lead)
    return total


def collide(pops, forces, rates, wanted):
    sums = [pops[a] + pops[b] for a, b in PAIRS]
    gaps = [pops[a] - pops[b] for a, b in PAIRS]
    density = pops[0]
    for entry in sums:
        density = density + entry
    momentum = [
        combine([VELOCITIES[a][axis] for a, _ in PAIRS], gaps) for axis in range(3)
    ]
    inverse = 1.0 / density
    force = [forces[axis] - forces[3] * (momentum[axis] * inverse) for axis in range(3)]
    velocity = [(momentum[axis] + 0.5 * force[axis]) * inverse for axis in range(3)]
    speed_sq = velocity[0] * velocity[0] + velocity[1] * velocity[1] + velocity[2] * velocity[2]
    u_dot_f = velocity[0] * force[0] + velocity[1] * force[1] + velocity[2] * force[2]
    base = 1.0 - 1.5 * speed_sq
    density_odd = 6.0 * density
    rest_source = (-3.0 * WEIGHTS[0]) * u_dot_f
    rest = pops[0] - WEIGHTS[0] * (density * base) + 0.5 * rest_source
    even_in, odd_in, even_source, odd_source = [rest], [], [], []
    for index, (a, _) in enumerate(PAIRS):
        along_u = combine(VELOCITIES[a], velocity)
        along_f = combine(VELOCITIES[a], force)
        weight = WEIGHTS[a]
        source_even = weight * (9.0 * along_u * along_f - 3.0 * u_dot_f)
        source_odd = (3.0 * weight) * along_f
        even_in.append(
            sums[index]
            - (2.0 * weight) * (density * (base + 4.5 * along_u * along_u))
            + source_even
        )
        odd_in.append(gaps[index] - weight * (density_odd * along_u) + source_odd)
        even_source.append(source_even)
        odd_source.append(source_odd)
    firsts = [a for a, _ in PAIRS]
    even_m = [rates[k] * combine(BASIS[k][[0] + firsts], even_in) for k in EVEN]
    odd_m = [rates[k] * combine(BASIS[k][firsts], odd_in) for k in ODD]
    out = {}
    if 0 in wanted:
        out[0] = pops[0] + rest_source - combine(BASIS[EVEN, 0], even_m)
    for index, (a, b) in enumerate(PAIRS):
        if a not in wanted and b not in wanted:
            continue
        even = even_source[index] - combine(BASIS[EVEN, a], even_m)
        odd = odd_source[index] - combine(BASIS[ODD, a], odd_m)
        out[a] = pops[a] + even + odd
        out[b] = pops[b] + even - odd
    return out


def lane_pick(row, lanes):
    table = jnp.broadcast_to(row, lanes.shape)
    return jnp.take_along_axis(table, lanes, axis=1, mode="promise_in_bounds")


def spread(values, rows, lanes, count):
    highs = [v.astype(jnp.bfloat16).astype(jnp.float32) for v in values]
    parts = highs + [v - h for v, h in zip(values, highs)]
    row_iota = lax.broadcasted_iota(jnp.int32, (count, 128), 0)
    lane_iota = lax.broadcasted_iota(jnp.int32, (128, 128), 0)
    left, right = [], []
    for s in range(8):
        hit = row_iota == rows[s : s + 1]
        left.append(
            jnp.concatenate(
                [jnp.where(hit, part[s : s + 1], 0.0) for part in parts], axis=0
            ).astype(jnp.bfloat16)
        )
        right.append(jnp.where(lane_iota == lanes[s : s + 1], 1.0, 0.0).astype(jnp.bfloat16))
    both = lax.dot_general(
        jnp.concatenate(left, axis=1),
        jnp.concatenate(right, axis=1),
        (((1,), (1,)), ((), ())),
        preferred_element_type=jnp.float32,
    )
    return both[: 4 * count] + both[4 * count :]


def kernel(
    devices_x,
    devices_z,
    pops_hbm,
    rates_hbm,
    wall_hbm,
    part_hbm,
    list_hbm,
    slot_hbm,
    cell_hbm,
    weight_hbm,
    out_ref,
    pops_ref,
    rates_ref,
    wall_ref,
    part_ref,
    list_ref,
    slot_ref,
    cell_ref,
    weight_ref,
    load_sem,
    stay,
    leave,
    arrive,
    values,
    force,
    plane_out,
    plane_in,
    edge_out,
    edge_in,
    corner_out,
    corner_in,
    coll,
    halo_x_out,
    halo_x_in,
    halo_z_out,
    halo_z_in,
    halo_c_in,
    solid,
    send_sem,
    recv_sem,
):
    me_x, me_z = lax.axis_index("gx"), lax.axis_index("gz")
    depth_z = 16
    rows_z = wall_ref.shape[0]

    def peer(step_x, step_z):
        return (
            lax.rem(me_x + step_x + devices_x, devices_x),
            lax.rem(me_z + step_z + devices_z, devices_z),
        )

    barrier = pltpu.get_barrier_semaphore()
    around = [(a, b) for a in (-1, 0, 1) for b in (-1, 0, 1) if (a, b) != (0, 0)]
    for step in around:
        pl.semaphore_signal(barrier, inc=1, device_id=peer(*step), device_id_type=MESH)

    loads = {}
    for at, (name, source, target) in enumerate(
        [
            ("list", list_hbm, list_ref),
            ("part", part_hbm, part_ref),
            ("slot", slot_hbm, slot_ref),
            ("weight", weight_hbm, weight_ref),
            ("cell", cell_hbm, cell_ref),
            ("wall", wall_hbm, wall_ref),
            ("rates", rates_hbm, rates_ref),
            ("pops", pops_hbm, pops_ref),
        ]
    ):
        loads[name] = pltpu.make_async_copy(source, target, load_sem.at[at])
        loads[name].start()

    count = [0]

    def send(source, target, step):
        at = count[0]
        count[0] += 1
        copy = pltpu.make_async_remote_copy(
            src_ref=source,
            dst_ref=target,
            send_sem=send_sem.at[at],
            recv_sem=recv_sem.at[at],
            device_id=peer(*step),
            device_id_type=MESH,
        )
        copy.start()
        return copy

    loads["list"].wait()
    loads["part"].wait()
    lists = list_ref[...]
    lists8 = jnp.concatenate([lists, lists], axis=0)
    list_hi, list_lo = lists8 >> 7, lists8 & 127
    picked = [jnp.zeros((8, 128), jnp.float32) for _ in range(4)]
    for h in range(16):
        hit = list_hi == h
        for c in range(4):
            picked[c] = jnp.where(
                hit, lane_pick(part_ref[c * 16 + h : c * 16 + h + 1], list_lo), picked[c]
            )
    for c in range(4):
        for d in range(4):
            leave[d, c : c + 1, :] = picked[c][d : d + 1]
    pl.semaphore_wait(barrier, len(around))
    migrations = [
        send(leave.at[d], arrive.at[d], step)
        for d, step in enumerate([(1, 0), (-1, 0), (0, 1), (0, -1)])
    ]

    hi_iota = lax.broadcasted_iota(jnp.int32, (16, 128), 0)
    lo_iota = lax.broadcasted_iota(jnp.int32, (128, 128), 0)
    left = jnp.concatenate(
        [jnp.where(hi_iota == list_hi[d : d + 1], 1.0, 0.0) for d in range(4)], axis=1
    ).astype(jnp.bfloat16)
    right = jnp.concatenate(
        [jnp.where(lo_iota == list_lo[d : d + 1], 1.0, 0.0) for d in range(4)], axis=1
    ).astype(jnp.bfloat16)
    gone = lax.dot_general(
        left, right, (((1,), (1,)), ((), ())), preferred_element_type=jnp.float32
    )
    for c in range(4):
        stay[c] = jnp.where(gone > 0.5, 0.0, part_ref[c * 16 : c * 16 + 16])

    def first_pick(j, carry):
        at = pl.ds(pl.multiple_of(j * 8, 8), 8)
        slots = slot_ref[at]
        hi, lo = slots >> 7, slots & 127
        got = [jnp.zeros((8, 128), jnp.float32) for _ in range(4)]
        for h in range(16):
            hit = hi == h
            for c in range(4):
                got[c] = jnp.where(hit, lane_pick(stay[c, h : h + 1], lo), got[c])
        for c in range(4):
            values[c, at] = got[c]
        return carry

    loads["slot"].wait()
    lax.fori_loop(0, 9, first_pick, 0)

    loads["wall"].wait()
    wall = jnp.where(
        (lax.broadcasted_iota(jnp.int32, (depth_z, 128), 1) == 0)
        | (lax.broadcasted_iota(jnp.int32, (depth_z, 128), 1) == 127),
        1,
        wall_ref[pl.ds(pl.multiple_of(me_z * depth_z, depth_z), depth_z)],
    )
    solid[PAD : PAD + depth_z] = wall
    lane = lax.broadcasted_iota(jnp.int32, (1, 128), 1)
    ends = (lane == 0) | (lane == 127)
    below = lax.rem(me_z * depth_z + rows_z - 1, rows_z)
    above = lax.rem(me_z * depth_z + depth_z, rows_z)
    solid[PAD - 1 : PAD] = jnp.where(ends, 1, wall_ref[pl.ds(below, 1)])
    solid[PAD + depth_z : PAD + depth_z + 1] = jnp.where(ends, 1, wall_ref[pl.ds(above, 1)])

    loads["weight"].wait()
    loads["cell"].wait()
    loads["rates"].wait()
    loads["pops"].wait()
    for copy in migrations:
        copy.wait()

    def second_pick(j, carry):
        at = pl.ds(j * 8 if isinstance(j, int) else pl.multiple_of(j * 8, 8), 8)
        slots = slot_ref[at]
        hi, lo = slots >> 7, slots & 127
        got = [values[c, at] for c in range(4)]
        for d in range(4):
            hit = hi == 16 + d
            for c in range(4):
                got[c] = jnp.where(hit, lane_pick(arrive[d, c : c + 1], lo), got[c])
        scale = weight_ref[at] * got[3]
        for c in range(3):
            values[c, at] = scale * got[c]
        values[3, at] = scale
        return carry

    def outer_pick(n, carry):
        return second_pick(jnp.where(n >= 4, n + 1, n), carry)

    lax.fori_loop(0, 8, outer_pick, 0)

    def bucket(step_x, step_z):
        at = ((step_x + 1) * 3 + step_z + 1) * 8
        cells = cell_ref[at : at + 8]
        return [values[c, at : at + 8] for c in range(4)], cells

    exchanges = []
    for s, step in enumerate(STEP):
        got, cells = bucket(step, 0)
        plane_out[s] = spread(got, (cells >> 7) & 15, cells & 127, 16).reshape(4, 16, 128)
        exchanges.append(send(plane_out.at[s], plane_in.at[s], (step, 0)))
    for s, step in enumerate(STEP):
        total = None
        for step_x in (-1, 0, 1):
            got, cells = bucket(step_x, step)
            rows = (cells >> 11) + 1 if step_x == 0 else jnp.full_like(cells, 0 if step_x < 0 else 5)
            part = spread(got, rows, cells & 127, 8)
            total = part if total is None else total + part
        edge_out[s] = total.reshape(4, 8, 128)
        exchanges.append(send(edge_out.at[s], edge_in.at[s], (0, step)))
        for sx, step_x in enumerate(STEP):
            at = s * 2 + sx
            row = 5 if step_x == 1 else 0
            for c in range(4):
                corner_out[at, c : c + 1] = total[c * 8 + row : c * 8 + row + 1]
            exchanges.append(send(corner_out.at[at], corner_in.at[at], (step_x, step)))
    second_pick(4, 0)
    got, cells = bucket(0, 0)
    force[...] = spread(got, cells >> 7, cells & 127, 64).reshape(4, 4, 16, 128)
    for copy in exchanges:
        copy.wait()
    for s in range(2):
        x = 0 if s == 0 else 3
        for c in range(4):
            force[c, x] = force[c, x] + plane_in[s, c]
    for s in range(2):
        z = 0 if s == 0 else 15
        for c in range(4):
            for x in range(4):
                row = edge_in[s, c, x + 1 : x + 2]
                if x == 0:
                    row = row + corner_in[s * 2, c : c + 1]
                if x == 3:
                    row = row + corner_in[s * 2 + 1, c : c + 1]
                force[c, x, z : z + 1] = force[c, x, z : z + 1] + row

    rates = [rates_ref[k] for k in range(19)]
    halos = []
    for x in (3, 0, 1, 2):
        done = collide(
            [pops_ref[q, x] for q in range(19)],
            [force[c, x] for c in range(4)],
            rates,
            range(19),
        )
        for q in range(19):
            coll[q, 1 + x, PAD : PAD + 16] = done[q]
        for s in range(2):
            z = 15 if s == 0 else 0
            for n, q in enumerate(ALONG_Z[s]):
                halo_z_out[s, n, x : x + 1] = done[q][z : z + 1]
        if x in (3, 0):
            s = 0 if x == 3 else 1
            for n, q in enumerate(ALONG_X[s]):
                halo_x_out[s, n] = done[q]
            halos.append(send(halo_x_out.at[s], halo_x_in.at[s], (STEP[s], 0)))
    for s in range(2):
        halos.append(send(halo_z_out.at[s], halo_z_in.at[s], (0, STEP[s])))
        for sx in range(2):
            q = VELOCITIES.index((STEP[sx], 0, STEP[s]))
            n = ALONG_Z[s].index(q)
            halos.append(
                send(halo_z_out.at[s, n], halo_c_in.at[s * 2 + sx], (STEP[sx], STEP[s]))
            )
    def stream(late):
        for q in range(19):
            step_x, step_y, step_z = VELOCITIES[q]
            for half in range(2):
                chosen = [
                    x
                    for x in range(4)
                    if late
                    == (
                        (step_x, x) in ((1, 0), (-1, 3)) or (step_z, half) in ((1, 0), (-1, 1))
                    )
                ]
                if not chosen:
                    continue
                at = PAD + 8 * half
                blocked = solid[at - step_z : at - step_z + 8]
                if step_y:
                    blocked = pltpu.roll(blocked, step_y % 128, 1)
                for x in chosen:
                    moved = coll[q, 1 + x - step_x, at - step_z : at - step_z + 8]
                    if step_y:
                        moved = pltpu.roll(moved, step_y % 128, 1)
                    out_ref[q, x, 8 * half : 8 * half + 8] = jnp.where(
                        blocked > 0, coll[OPPOSITE[q], 1 + x, at : at + 8], moved
                    )

    stream(False)
    for copy in halos:
        copy.wait()
    for s in range(2):
        for n, q in enumerate(ALONG_X[s]):
            coll[q, 0 if s == 0 else 5, PAD : PAD + 16] = halo_x_in[s, n]
        z = PAD - 1 if s == 0 else PAD + 16
        for n, q in enumerate(ALONG_Z[s]):
            for x in range(4):
                coll[q, 1 + x, z : z + 1] = halo_z_in[s, n, x : x + 1]
        for sx in range(2):
            q = VELOCITIES.index((STEP[sx], 0, STEP[s]))
            x = 3 if sx == 0 else 0
            coll[q, 0 if sx == 0 else 5, z : z + 1] = halo_c_in[s * 2 + sx, x : x + 1]

    stream(True)


def solution(mesh):
    devices_x, devices_z = mesh.shape["gx"], mesh.shape["gz"]

    def body(pops, rates, wall, particles, lists, slot, cell, weight):
        vmem = pl.BlockSpec(memory_space=pltpu.VMEM)
        hbm = pl.BlockSpec(memory_space=pltpu.HBM)
        f32 = jnp.float32
        return pl.pallas_call(
            lambda *refs: kernel(devices_x, devices_z, *refs),
            out_shape=jax.ShapeDtypeStruct(pops.shape, f32),
            in_specs=[hbm] * 8,
            out_specs=vmem,
            scratch_shapes=[
                pltpu.VMEM(pops.shape, f32),
                pltpu.SMEM(rates.shape, f32),
                pltpu.VMEM(wall.shape, jnp.int32),
                pltpu.VMEM((64, 128), f32),
                pltpu.VMEM((4, 128), jnp.int32),
                pltpu.VMEM((72, 128), jnp.int32),
                pltpu.VMEM((72, 128), jnp.int32),
                pltpu.VMEM((72, 128), f32),
                pltpu.SemaphoreType.DMA((8,)),
                pltpu.VMEM((4, 16, 128), f32),
                pltpu.VMEM((4, 8, 128), f32),
                pltpu.VMEM((4, 8, 128), f32),
                pltpu.VMEM((4, 72, 128), f32),
                pltpu.VMEM((4, 4, 16, 128), f32),
                pltpu.VMEM((2, 4, 16, 128), f32),
                pltpu.VMEM((2, 4, 16, 128), f32),
                pltpu.VMEM((2, 4, 8, 128), f32),
                pltpu.VMEM((2, 4, 8, 128), f32),
                pltpu.VMEM((4, 4, 128), f32),
                pltpu.VMEM((4, 4, 128), f32),
                pltpu.VMEM((19, 6, 32, 128), f32),
                pltpu.VMEM((2, 5, 16, 128), f32),
                pltpu.VMEM((2, 5, 16, 128), f32),
                pltpu.VMEM((2, 5, 8, 128), f32),
                pltpu.VMEM((2, 5, 8, 128), f32),
                pltpu.VMEM((4, 8, 128), f32),
                pltpu.VMEM((32, 128), jnp.int32),
                pltpu.SemaphoreType.DMA((20,)),
                pltpu.SemaphoreType.DMA((20,)),
            ],
            compiler_params=pltpu.CompilerParams(
                collective_id=0, has_side_effects=True, vmem_limit_bytes=56000 * 1024
            ),
        )(
            pops,
            rates,
            wall,
            particles.reshape(64, 128),
            lists.reshape(4, 128),
            slot.reshape(72, 128),
            cell.reshape(72, 128),
            weight.reshape(72, 128),
        )

    return jax.shard_map(
        body,
        mesh=mesh,
        in_specs=(
            P(None, "gx", "gz", None),
            P(),
            P(),
            P(None, "gx", "gz", None),
            P("gx", "gz", None, None),
            P("gx", "gz", None, None),
            P("gx", "gz", None, None),
            P("gx", "gz", None, None),
        ),
        out_specs=P(None, "gx", "gz", None),
        check_vma=False,
    )
```

```python
import jax
import jax.numpy as jnp
import numpy as np
from jax import lax
from jax.experimental import pallas as pl
from jax.experimental.pallas import tpu as pltpu
from jax.sharding import PartitionSpec as P

MESH = pl.DeviceIdType.MESH
VELOCITIES = [
    (0, 0, 0),
    (1, 0, 0),
    (-1, 0, 0),
    (0, 1, 0),
    (0, -1, 0),
    (0, 0, 1),
    (0, 0, -1),
    (1, 1, 0),
    (-1, -1, 0),
    (1, -1, 0),
    (-1, 1, 0),
    (1, 0, 1),
    (-1, 0, -1),
    (1, 0, -1),
    (-1, 0, 1),
    (0, 1, 1),
    (0, -1, -1),
    (0, 1, -1),
    (0, -1, 1),
]
WEIGHTS = [1.0 / 3.0] + [1.0 / 18.0] * 6 + [1.0 / 36.0] * 12
OPPOSITE = [VELOCITIES.index((-a, -b, -c)) for a, b, c in VELOCITIES]
PAIRS = [(q, OPPOSITE[q]) for q in range(1, 19) if q < OPPOSITE[q]]
ALONG_X = [[q for q in range(19) if VELOCITIES[q][0] == s] for s in (1, -1)]
ALONG_Z = [[q for q in range(19) if VELOCITIES[q][2] == s] for s in (1, -1)]
STEP = (1, -1)
CORNERS = [(0, 0), (0, 1), (1, 0), (1, 1)]
PAD = 8


def moment_basis():
    table = np.array(VELOCITIES) * 1.0
    x, y, z = table[:, 0], table[:, 1], table[:, 2]
    square = x * x + y * y + z * z
    raw_list = [
        np.ones(19),
        square,
        square * square,
        x,
        y,
        z,
        square * x,
        square * y,
        square * z,
        3 * x * x - square,
        square * (3 * x * x - square),
        y * y - z * z,
        square * (y * y - z * z),
        x * y,
        y * z,
        x * z,
        x * (y * y - z * z),
        y * (z * z - x * x),
        z * (x * x - y * y),
    ]
    basis = []
    for vector in raw_list:
        for earlier in basis:
            vector = vector - np.dot(vector, earlier) * earlier
        basis.append(vector / np.sqrt(np.dot(vector, vector)))
    return np.stack(basis)


BASIS = moment_basis()
EVEN = [1, 2, 9, 10, 11, 12, 13, 14, 15]
ODD = [6, 7, 8, 16, 17, 18]


def combine(coefficients, values):
    groups = {}
    for coefficient, value in zip(coefficients, values):
        if abs(coefficient) < 1e-9:
            continue
        groups.setdefault(round(abs(coefficient), 9), []).append((float(coefficient), value))
    total = None
    for members in groups.values():
        size = abs(members[0][0])
        lead = 1.0 if members[0][0] > 0 else -1.0
        part = members[0][1]
        for coefficient, value in members[1:]:
            part = part + value if coefficient * lead > 0 else part - value
        if total is None:
            total = part * (size * lead)
        else:
            total = total + part * (size * lead)
    return total


def collide(pops, forces, rates, wanted):
    sums = [pops[a] + pops[b] for a, b in PAIRS]
    gaps = [pops[a] - pops[b] for a, b in PAIRS]
    density = pops[0]
    for entry in sums:
        density = density + entry
    momentum = [
        combine([VELOCITIES[a][axis] for a, _ in PAIRS], gaps) for axis in range(3)
    ]
    inverse = 1.0 / density
    force = [forces[axis] - forces[3] * (momentum[axis] * inverse) for axis in range(3)]
    velocity = [(momentum[axis] + 0.5 * force[axis]) * inverse for axis in range(3)]
    speed_sq = velocity[0] * velocity[0] + velocity[1] * velocity[1] + velocity[2] * velocity[2]
    u_dot_f = velocity[0] * force[0] + velocity[1] * force[1] + velocity[2] * force[2]
    base = 1.0 - 1.5 * speed_sq
    density_odd = 6.0 * density
    rest_source = (-3.0 * WEIGHTS[0]) * u_dot_f
    rest = pops[0] - WEIGHTS[0] * (density * base) + 0.5 * rest_source
    even_in, odd_in, even_source, odd_source = [rest], [], [], []
    for index, (a, _) in enumerate(PAIRS):
        along_u = combine(VELOCITIES[a], velocity)
        along_f = combine(VELOCITIES[a], force)
        weight = WEIGHTS[a]
        source_even = weight * (9.0 * along_u * along_f - 3.0 * u_dot_f)
        source_odd = (3.0 * weight) * along_f
        even_in.append(
            sums[index]
            - (2.0 * weight) * (density * (base + 4.5 * along_u * along_u))
            + source_even
        )
        odd_in.append(gaps[index] - weight * (density_odd * along_u) + source_odd)
        even_source.append(source_even)
        odd_source.append(source_odd)
    firsts = [a for a, _ in PAIRS]
    even_m = [rates[k] * combine(BASIS[k][[0] + firsts], even_in) for k in EVEN]
    odd_m = [rates[k] * combine(BASIS[k][firsts], odd_in) for k in ODD]
    out = {}
    if 0 in wanted:
        out[0] = pops[0] + rest_source - combine(BASIS[EVEN, 0], even_m)
    for index, (a, b) in enumerate(PAIRS):
        if a not in wanted and b not in wanted:
            continue
        even = even_source[index] - combine(BASIS[EVEN, a], even_m)
        odd = odd_source[index] - combine(BASIS[ODD, a], odd_m)
        out[a] = pops[a] + even + odd
        out[b] = pops[b] + even - odd
    return out


def lane_pick(row, lanes):
    table = jnp.broadcast_to(row, lanes.shape)
    return jnp.take_along_axis(table, lanes, axis=1, mode="promise_in_bounds")


def spread(values, rows, lanes, count):
    highs = [v.astype(jnp.bfloat16).astype(jnp.float32) for v in values]
    parts = highs + [v - h for v, h in zip(values, highs)]
    row_iota = lax.broadcasted_iota(jnp.int32, (count, 128), 0)
    lane_iota = lax.broadcasted_iota(jnp.int32, (128, 128), 0)
    left, right = [], []
    for s in range(8):
        hit = row_iota == rows[s : s + 1]
        left.append(
            jnp.concatenate(
                [jnp.where(hit, part[s : s + 1], 0.0) for part in parts], axis=0
            ).astype(jnp.bfloat16)
        )
        right.append(jnp.where(lane_iota == lanes[s : s + 1], 1.0, 0.0).astype(jnp.bfloat16))
    both = lax.dot_general(
        jnp.concatenate(left, axis=1),
        jnp.concatenate(right, axis=1),
        (((1,), (1,)), ((), ())),
        preferred_element_type=jnp.float32,
    )
    return both[: 4 * count] + both[4 * count :]


def kernel(
    devices_x,
    devices_z,
    pops_hbm,
    rates_hbm,
    wall_hbm,
    part_hbm,
    list_hbm,
    slot_hbm,
    cell_hbm,
    weight_hbm,
    out_ref,
    pops_ref,
    rates_ref,
    wall_ref,
    part_ref,
    list_ref,
    slot_ref,
    cell_ref,
    weight_ref,
    load_sem,
    stay,
    leave,
    arrive,
    values,
    force,
    plane_out,
    plane_in,
    edge_out,
    edge_in,
    corner_out,
    corner_in,
    coll,
    halo_x_out,
    halo_x_in,
    halo_z_out,
    halo_z_in,
    halo_c_in,
    solid,
    send_sem,
    recv_sem,
):
    me_x, me_z = lax.axis_index("gx"), lax.axis_index("gz")
    depth_z = 16
    rows_z = wall_ref.shape[0]

    def peer(step_x, step_z):
        return (
            lax.rem(me_x + step_x + devices_x, devices_x),
            lax.rem(me_z + step_z + devices_z, devices_z),
        )

    barrier = pltpu.get_barrier_semaphore()
    around = [(a, b) for a in (-1, 0, 1) for b in (-1, 0, 1) if (a, b) != (0, 0)]
    for step in around:
        pl.semaphore_signal(barrier, inc=1, device_id=peer(*step), device_id_type=MESH)

    loads = {}
    for at, (name, source, target) in enumerate(
        [
            ("list", list_hbm, list_ref),
            ("part", part_hbm, part_ref),
            ("slot", slot_hbm, slot_ref),
            ("weight", weight_hbm, weight_ref),
            ("cell", cell_hbm, cell_ref),
            ("wall", wall_hbm, wall_ref),
            ("rates", rates_hbm, rates_ref),
            ("pops", pops_hbm, pops_ref),
        ]
    ):
        loads[name] = pltpu.make_async_copy(source, target, load_sem.at[at])
        loads[name].start()

    count = [0]

    def send(source, target, step):
        at = count[0]
        count[0] += 1
        copy = pltpu.make_async_remote_copy(
            src_ref=source,
            dst_ref=target,
            send_sem=send_sem.at[at],
            recv_sem=recv_sem.at[at],
            device_id=peer(*step),
            device_id_type=MESH,
        )
        copy.start()
        return copy

    loads["list"].wait()
    loads["part"].wait()
    lists = list_ref[...]
    lists8 = jnp.concatenate([lists, lists], axis=0)
    list_hi, list_lo = lists8 >> 7, lists8 & 127
    picked = [jnp.zeros((8, 128), jnp.float32) for _ in range(4)]
    for h in range(16):
        hit = list_hi == h
        for c in range(4):
            picked[c] = jnp.where(
                hit, lane_pick(part_ref[c * 16 + h : c * 16 + h + 1], list_lo), picked[c]
            )
    for c in range(4):
        for d in range(4):
            leave[d, c : c + 1, :] = picked[c][d : d + 1]
    pl.semaphore_wait(barrier, len(around))
    migrations = [
        send(leave.at[d], arrive.at[d], step)
        for d, step in enumerate([(1, 0), (-1, 0), (0, 1), (0, -1)])
    ]

    hi_iota = lax.broadcasted_iota(jnp.int32, (16, 128), 0)
    lo_iota = lax.broadcasted_iota(jnp.int32, (128, 128), 0)
    left = jnp.concatenate(
        [jnp.where(hi_iota == list_hi[d : d + 1], 1.0, 0.0) for d in range(4)], axis=1
    ).astype(jnp.bfloat16)
    right = jnp.concatenate(
        [jnp.where(lo_iota == list_lo[d : d + 1], 1.0, 0.0) for d in range(4)], axis=1
    ).astype(jnp.bfloat16)
    gone = lax.dot_general(
        left, right, (((1,), (1,)), ((), ())), preferred_element_type=jnp.float32
    )
    for c in range(4):
        stay[c] = jnp.where(gone > 0.5, 0.0, part_ref[c * 16 : c * 16 + 16])

    def first_pick(j, carry):
        at = pl.ds(pl.multiple_of(j * 8, 8), 8)
        slots = slot_ref[at]
        hi, lo = slots >> 7, slots & 127
        got = [jnp.zeros((8, 128), jnp.float32) for _ in range(4)]
        for h in range(16):
            hit = hi == h
            for c in range(4):
                got[c] = jnp.where(hit, lane_pick(stay[c, h : h + 1], lo), got[c])
        for c in range(4):
            values[c, at] = got[c]
        return carry

    loads["slot"].wait()
    lax.fori_loop(0, 9, first_pick, 0)

    loads["wall"].wait()
    wall = jnp.where(
        (lax.broadcasted_iota(jnp.int32, (depth_z, 128), 1) == 0)
        | (lax.broadcasted_iota(jnp.int32, (depth_z, 128), 1) == 127),
        1,
        wall_ref[pl.ds(pl.multiple_of(me_z * depth_z, depth_z), depth_z)],
    )
    solid[PAD : PAD + depth_z] = wall
    lane = lax.broadcasted_iota(jnp.int32, (1, 128), 1)
    ends = (lane == 0) | (lane == 127)
    below = lax.rem(me_z * depth_z + rows_z - 1, rows_z)
    above = lax.rem(me_z * depth_z + depth_z, rows_z)
    solid[PAD - 1 : PAD] = jnp.where(ends, 1, wall_ref[pl.ds(below, 1)])
    solid[PAD + depth_z : PAD + depth_z + 1] = jnp.where(ends, 1, wall_ref[pl.ds(above, 1)])

    loads["weight"].wait()
    loads["cell"].wait()
    loads["rates"].wait()
    loads["pops"].wait()
    for copy in migrations:
        copy.wait()

    def second_pick(j, carry):
        at = pl.ds(j * 8 if isinstance(j, int) else pl.multiple_of(j * 8, 8), 8)
        slots = slot_ref[at]
        hi, lo = slots >> 7, slots & 127
        got = [values[c, at] for c in range(4)]
        for d in range(4):
            hit = hi == 16 + d
            for c in range(4):
                got[c] = jnp.where(hit, lane_pick(arrive[d, c : c + 1], lo), got[c])
        scale = weight_ref[at] * got[3]
        for c in range(3):
            values[c, at] = scale * got[c]
        values[3, at] = scale
        return carry

    def outer_pick(n, carry):
        return second_pick(jnp.where(n >= 4, n + 1, n), carry)

    lax.fori_loop(0, 8, outer_pick, 0)

    def bucket(step_x, step_z):
        at = ((step_x + 1) * 3 + step_z + 1) * 8
        cells = cell_ref[at : at + 8]
        return [values[c, at : at + 8] for c in range(4)], cells

    exchanges = []
    for s, step in enumerate(STEP):
        got, cells = bucket(step, 0)
        plane_out[s] = spread(got, (cells >> 7) & 15, cells & 127, 16).reshape(4, 16, 128)
        exchanges.append(send(plane_out.at[s], plane_in.at[s], (step, 0)))
    for s, step in enumerate(STEP):
        total = None
        for step_x in (-1, 0, 1):
            got, cells = bucket(step_x, step)
            rows = (cells >> 11) + 1 if step_x == 0 else jnp.full_like(cells, 0 if step_x < 0 else 5)
            part = spread(got, rows, cells & 127, 8)
            total = part if total is None else total + part
        edge_out[s] = total.reshape(4, 8, 128)
        exchanges.append(send(edge_out.at[s], edge_in.at[s], (0, step)))
        for sx, step_x in enumerate(STEP):
            at = s * 2 + sx
            row = 5 if step_x == 1 else 0
            for c in range(4):
                corner_out[at, c : c + 1] = total[c * 8 + row : c * 8 + row + 1]
            exchanges.append(send(corner_out.at[at], corner_in.at[at], (step_x, step)))
    second_pick(4, 0)
    got, cells = bucket(0, 0)
    force[...] = spread(got, cells >> 7, cells & 127, 64).reshape(4, 4, 16, 128)
    for copy in exchanges:
        copy.wait()
    for s in range(2):
        x = 0 if s == 0 else 3
        for c in range(4):
            force[c, x] = force[c, x] + plane_in[s, c]
    for s in range(2):
        z = 0 if s == 0 else 15
        for c in range(4):
            for x in range(4):
                row = edge_in[s, c, x + 1 : x + 2]
                if x == 0:
                    row = row + corner_in[s * 2, c : c + 1]
                if x == 3:
                    row = row + corner_in[s * 2 + 1, c : c + 1]
                force[c, x, z : z + 1] = force[c, x, z : z + 1] + row

    rates = [rates_ref[k] for k in range(19)]
    halos = []
    for x in (3, 0, 1, 2):
        done = collide(
            [pops_ref[q, x] for q in range(19)],
            [force[c, x] for c in range(4)],
            rates,
            range(19),
        )
        for q in range(19):
            coll[q, 1 + x, PAD : PAD + 16] = done[q]
        for s in range(2):
            z = 15 if s == 0 else 0
            for n, q in enumerate(ALONG_Z[s]):
                halo_z_out[s, n, x : x + 1] = done[q][z : z + 1]
        if x in (3, 0):
            s = 0 if x == 3 else 1
            for n, q in enumerate(ALONG_X[s]):
                halo_x_out[s, n] = done[q]
            halos.append(send(halo_x_out.at[s], halo_x_in.at[s], (STEP[s], 0)))
    for s in range(2):
        halos.append(send(halo_z_out.at[s], halo_z_in.at[s], (0, STEP[s])))
        for sx in range(2):
            q = VELOCITIES.index((STEP[sx], 0, STEP[s]))
            n = ALONG_Z[s].index(q)
            halos.append(
                send(halo_z_out.at[s, n], halo_c_in.at[s * 2 + sx], (STEP[sx], STEP[s]))
            )
    def stream(late):
        for q in range(19):
            step_x, step_y, step_z = VELOCITIES[q]
            for half in range(2):
                chosen = [
                    x
                    for x in range(4)
                    if late
                    == (
                        (step_x, x) in ((1, 0), (-1, 3)) or (step_z, half) in ((1, 0), (-1, 1))
                    )
                ]
                if not chosen:
                    continue
                at = PAD + 8 * half
                blocked = solid[at - step_z : at - step_z + 8]
                if step_y:
                    blocked = pltpu.roll(blocked, step_y % 128, 1)
                for x in chosen:
                    moved = coll[q, 1 + x - step_x, at - step_z : at - step_z + 8]
                    if step_y:
                        moved = pltpu.roll(moved, step_y % 128, 1)
                    out_ref[q, x, 8 * half : 8 * half + 8] = jnp.where(
                        blocked > 0, coll[OPPOSITE[q], 1 + x, at : at + 8], moved
                    )

    stream(False)
    for copy in halos:
        copy.wait()
    for s in range(2):
        for n, q in enumerate(ALONG_X[s]):
            coll[q, 0 if s == 0 else 5, PAD : PAD + 16] = halo_x_in[s, n]
        z = PAD - 1 if s == 0 else PAD + 16
        for n, q in enumerate(ALONG_Z[s]):
            for x in range(4):
                coll[q, 1 + x, z : z + 1] = halo_z_in[s, n, x : x + 1]
        for sx in range(2):
            q = VELOCITIES.index((STEP[sx], 0, STEP[s]))
            x = 3 if sx == 0 else 0
            coll[q, 0 if sx == 0 else 5, z : z + 1] = halo_c_in[s * 2 + sx, x : x + 1]

    stream(True)


def solution(mesh):
    devices_x, devices_z = mesh.shape["gx"], mesh.shape["gz"]

    def body(pops, rates, wall, particles, lists, slot, cell, weight):
        vmem = pl.BlockSpec(memory_space=pltpu.VMEM)
        hbm = pl.BlockSpec(memory_space=pltpu.HBM)
        f32 = jnp.float32
        return pl.pallas_call(
            lambda *refs: kernel(devices_x, devices_z, *refs),
            out_shape=pltpu.VMEM(pops.shape, f32),
            in_specs=[hbm] * 8,
            out_specs=vmem,
            scratch_shapes=[
                pltpu.VMEM(pops.shape, f32),
                pltpu.SMEM(rates.shape, f32),
                pltpu.VMEM(wall.shape, jnp.int32),
                pltpu.VMEM((64, 128), f32),
                pltpu.VMEM((4, 128), jnp.int32),
                pltpu.VMEM((72, 128), jnp.int32),
                pltpu.VMEM((72, 128), jnp.int32),
                pltpu.VMEM((72, 128), f32),
                pltpu.SemaphoreType.DMA((8,)),
                pltpu.VMEM((4, 16, 128), f32),
                pltpu.VMEM((4, 8, 128), f32),
                pltpu.VMEM((4, 8, 128), f32),
                pltpu.VMEM((4, 72, 128), f32),
                pltpu.VMEM((4, 4, 16, 128), f32),
                pltpu.VMEM((2, 4, 16, 128), f32),
                pltpu.VMEM((2, 4, 16, 128), f32),
                pltpu.VMEM((2, 4, 8, 128), f32),
                pltpu.VMEM((2, 4, 8, 128), f32),
                pltpu.VMEM((4, 4, 128), f32),
                pltpu.VMEM((4, 4, 128), f32),
                pltpu.VMEM((19, 6, 32, 128), f32),
                pltpu.VMEM((2, 5, 16, 128), f32),
                pltpu.VMEM((2, 5, 16, 128), f32),
                pltpu.VMEM((2, 5, 8, 128), f32),
                pltpu.VMEM((2, 5, 8, 128), f32),
                pltpu.VMEM((4, 8, 128), f32),
                pltpu.VMEM((32, 128), jnp.int32),
                pltpu.SemaphoreType.DMA((20,)),
                pltpu.SemaphoreType.DMA((20,)),
            ],
            compiler_params=pltpu.CompilerParams(
                collective_id=0, has_side_effects=True, vmem_limit_bytes=56000 * 1024
            ),
        )(
            pops,
            rates,
            wall,
            particles.reshape(64, 128),
            lists.reshape(4, 128),
            slot.reshape(72, 128),
            cell.reshape(72, 128),
            weight.reshape(72, 128),
        )

    return jax.shard_map(
        body,
        mesh=mesh,
        in_specs=(
            P(None, "gx", "gz", None),
            P(),
            P(),
            P(None, "gx", "gz", None),
            P("gx", "gz", None, None),
            P("gx", "gz", None, None),
            P("gx", "gz", None, None),
            P("gx", "gz", None, None),
        ),
        out_specs=P(None, "gx", "gz", None),
        check_vma=False,
    )
```

```python
import jax
import jax.numpy as jnp
import numpy as np
from jax import lax
from jax.experimental import pallas as pl
from jax.experimental.pallas import tpu as pltpu
from jax.sharding import PartitionSpec as P

MESH = pl.DeviceIdType.MESH
VELOCITIES = [
    (0, 0, 0),
    (1, 0, 0),
    (-1, 0, 0),
    (0, 1, 0),
    (0, -1, 0),
    (0, 0, 1),
    (0, 0, -1),
    (1, 1, 0),
    (-1, -1, 0),
    (1, -1, 0),
    (-1, 1, 0),
    (1, 0, 1),
    (-1, 0, -1),
    (1, 0, -1),
    (-1, 0, 1),
    (0, 1, 1),
    (0, -1, -1),
    (0, 1, -1),
    (0, -1, 1),
]
WEIGHTS = [1.0 / 3.0] + [1.0 / 18.0] * 6 + [1.0 / 36.0] * 12
OPPOSITE = [VELOCITIES.index((-a, -b, -c)) for a, b, c in VELOCITIES]
PAIRS = [(q, OPPOSITE[q]) for q in range(1, 19) if q < OPPOSITE[q]]
ALONG_X = [[q for q in range(19) if VELOCITIES[q][0] == s] for s in (1, -1)]
ALONG_Z = [[q for q in range(19) if VELOCITIES[q][2] == s] for s in (1, -1)]
STEP = (1, -1)
CORNERS = [(0, 0), (0, 1), (1, 0), (1, 1)]
PAD = 8


def moment_basis():
    table = np.array(VELOCITIES) * 1.0
    x, y, z = table[:, 0], table[:, 1], table[:, 2]
    square = x * x + y * y + z * z
    raw_list = [
        np.ones(19),
        square,
        square * square,
        x,
        y,
        z,
        square * x,
        square * y,
        square * z,
        3 * x * x - square,
        square * (3 * x * x - square),
        y * y - z * z,
        square * (y * y - z * z),
        x * y,
        y * z,
        x * z,
        x * (y * y - z * z),
        y * (z * z - x * x),
        z * (x * x - y * y),
    ]
    basis = []
    for vector in raw_list:
        for earlier in basis:
            vector = vector - np.dot(vector, earlier) * earlier
        basis.append(vector / np.sqrt(np.dot(vector, vector)))
    return np.stack(basis)


BASIS = moment_basis()
EVEN = [1, 2, 9, 10, 11, 12, 13, 14, 15]
ODD = [6, 7, 8, 16, 17, 18]


def combine(coefficients, values):
    groups = {}
    for coefficient, value in zip(coefficients, values):
        if abs(coefficient) < 1e-9:
            continue
        groups.setdefault(round(abs(coefficient), 9), []).append((float(coefficient), value))
    total = None
    for members in groups.values():
        size = abs(members[0][0])
        lead = 1.0 if members[0][0] > 0 else -1.0
        part = members[0][1]
        for coefficient, value in members[1:]:
            part = part + value if coefficient * lead > 0 else part - value
        if total is None:
            total = part * (size * lead)
        else:
            total = total + part * (size * lead)
    return total


def collide(pops, forces, rates, wanted):
    sums = [pops[a] + pops[b] for a, b in PAIRS]
    gaps = [pops[a] - pops[b] for a, b in PAIRS]
    density = pops[0]
    for entry in sums:
        density = density + entry
    momentum = [
        combine([VELOCITIES[a][axis] for a, _ in PAIRS], gaps) for axis in range(3)
    ]
    inverse = 1.0 / density
    force = [forces[axis] - forces[3] * (momentum[axis] * inverse) for axis in range(3)]
    velocity = [(momentum[axis] + 0.5 * force[axis]) * inverse for axis in range(3)]
    speed_sq = velocity[0] * velocity[0] + velocity[1] * velocity[1] + velocity[2] * velocity[2]
    u_dot_f = velocity[0] * force[0] + velocity[1] * force[1] + velocity[2] * force[2]
    base = 1.0 - 1.5 * speed_sq
    density_odd = 6.0 * density
    rest_source = (-3.0 * WEIGHTS[0]) * u_dot_f
    rest = pops[0] - WEIGHTS[0] * (density * base) + 0.5 * rest_source
    even_in, odd_in, even_source, odd_source = [rest], [], [], []
    for index, (a, _) in enumerate(PAIRS):
        along_u = combine(VELOCITIES[a], velocity)
        along_f = combine(VELOCITIES[a], force)
        weight = WEIGHTS[a]
        source_even = weight * (9.0 * along_u * along_f - 3.0 * u_dot_f)
        source_odd = (3.0 * weight) * along_f
        even_in.append(
            sums[index]
            - (2.0 * weight) * (density * (base + 4.5 * along_u * along_u))
            + source_even
        )
        odd_in.append(gaps[index] - weight * (density_odd * along_u) + source_odd)
        even_source.append(source_even)
        odd_source.append(source_odd)
    firsts = [a for a, _ in PAIRS]
    even_m = [rates[k] * combine(BASIS[k][[0] + firsts], even_in) for k in EVEN]
    odd_m = [rates[k] * combine(BASIS[k][firsts], odd_in) for k in ODD]
    out = {}
    if 0 in wanted:
        out[0] = pops[0] + rest_source - combine(BASIS[EVEN, 0], even_m)
    for index, (a, b) in enumerate(PAIRS):
        if a not in wanted and b not in wanted:
            continue
        even = even_source[index] - combine(BASIS[EVEN, a], even_m)
        odd = odd_source[index] - combine(BASIS[ODD, a], odd_m)
        out[a] = pops[a] + even + odd
        out[b] = pops[b] + even - odd
    return out


def lane_pick(row, lanes):
    table = jnp.broadcast_to(row, lanes.shape)
    return jnp.take_along_axis(table, lanes, axis=1, mode="promise_in_bounds")


def spread(values, rows, lanes, count):
    highs = [v.astype(jnp.bfloat16).astype(jnp.float32) for v in values]
    parts = highs + [v - h for v, h in zip(values, highs)]
    row_iota = lax.broadcasted_iota(jnp.int32, (count, 128), 0)
    lane_iota = lax.broadcasted_iota(jnp.int32, (128, 128), 0)
    left, right = [], []
    for s in range(8):
        hit = row_iota == rows[s : s + 1]
        left.append(
            jnp.concatenate(
                [jnp.where(hit, part[s : s + 1], 0.0) for part in parts], axis=0
            ).astype(jnp.bfloat16)
        )
        right.append(jnp.where(lane_iota == lanes[s : s + 1], 1.0, 0.0).astype(jnp.bfloat16))
    both = lax.dot_general(
        jnp.concatenate(left, axis=1),
        jnp.concatenate(right, axis=1),
        (((1,), (1,)), ((), ())),
        preferred_element_type=jnp.float32,
    )
    return both[: 4 * count] + both[4 * count :]


def kernel(
    devices_x,
    devices_z,
    pops_hbm,
    rates_hbm,
    wall_hbm,
    part_hbm,
    list_hbm,
    slot_hbm,
    cell_hbm,
    weight_hbm,
    out_ref,
    pops_ref,
    rates_ref,
    wall_ref,
    part_ref,
    list_ref,
    slot_ref,
    cell_ref,
    weight_ref,
    load_sem,
    stay,
    leave,
    arrive,
    values,
    force,
    plane_out,
    plane_in,
    edge_out,
    edge_in,
    corner_out,
    corner_in,
    coll,
    halo_x_out,
    halo_x_in,
    halo_z_out,
    halo_z_in,
    halo_c_out,
    halo_c_in,
    solid,
    send_sem,
    recv_sem,
):
    me_x, me_z = lax.axis_index("gx"), lax.axis_index("gz")
    depth_z = 16
    rows_z = wall_ref.shape[0]

    def peer(step_x, step_z):
        return (
            lax.rem(me_x + step_x + devices_x, devices_x),
            lax.rem(me_z + step_z + devices_z, devices_z),
        )

    barrier = pltpu.get_barrier_semaphore()
    around = [(a, b) for a in (-1, 0, 1) for b in (-1, 0, 1) if (a, b) != (0, 0)]
    for step in around:
        pl.semaphore_signal(barrier, inc=1, device_id=peer(*step), device_id_type=MESH)

    loads = {}
    for at, (name, source, target) in enumerate(
        [
            ("list", list_hbm, list_ref),
            ("part", part_hbm, part_ref),
            ("slot", slot_hbm, slot_ref),
            ("weight", weight_hbm, weight_ref),
            ("cell", cell_hbm, cell_ref),
            ("wall", wall_hbm, wall_ref),
            ("rates", rates_hbm, rates_ref),
            ("pops", pops_hbm, pops_ref),
        ]
    ):
        loads[name] = pltpu.make_async_copy(source, target, load_sem.at[at])
        loads[name].start()

    count = [0]

    def send(source, target, step):
        at = count[0]
        count[0] += 1
        copy = pltpu.make_async_remote_copy(
            src_ref=source,
            dst_ref=target,
            send_sem=send_sem.at[at],
            recv_sem=recv_sem.at[at],
            device_id=peer(*step),
            device_id_type=MESH,
        )
        copy.start()
        return copy

    loads["list"].wait()
    loads["part"].wait()
    lists = list_ref[...]
    lists8 = jnp.concatenate([lists, lists], axis=0)
    list_hi, list_lo = lists8 >> 7, lists8 & 127
    picked = [jnp.zeros((8, 128), jnp.float32) for _ in range(4)]
    for h in range(16):
        hit = list_hi == h
        for c in range(4):
            picked[c] = jnp.where(
                hit, lane_pick(part_ref[c * 16 + h : c * 16 + h + 1], list_lo), picked[c]
            )
    for c in range(4):
        for d in range(4):
            leave[d, c : c + 1, :] = picked[c][d : d + 1]
    pl.semaphore_wait(barrier, len(around))
    migrations = [
        send(leave.at[d], arrive.at[d], step)
        for d, step in enumerate([(1, 0), (-1, 0), (0, 1), (0, -1)])
    ]

    hi_iota = lax.broadcasted_iota(jnp.int32, (16, 128), 0)
    lo_iota = lax.broadcasted_iota(jnp.int32, (128, 128), 0)
    left = jnp.concatenate(
        [jnp.where(hi_iota == list_hi[d : d + 1], 1.0, 0.0) for d in range(4)], axis=1
    ).astype(jnp.bfloat16)
    right = jnp.concatenate(
        [jnp.where(lo_iota == list_lo[d : d + 1], 1.0, 0.0) for d in range(4)], axis=1
    ).astype(jnp.bfloat16)
    gone = lax.dot_general(
        left, right, (((1,), (1,)), ((), ())), preferred_element_type=jnp.float32
    )
    for c in range(4):
        stay[c] = jnp.where(gone > 0.5, 0.0, part_ref[c * 16 : c * 16 + 16])

    def first_pick(j, carry):
        at = pl.ds(pl.multiple_of(j * 8, 8), 8)
        slots = slot_ref[at]
        hi, lo = slots >> 7, slots & 127
        got = [jnp.zeros((8, 128), jnp.float32) for _ in range(4)]
        for h in range(16):
            hit = hi == h
            for c in range(4):
                got[c] = jnp.where(hit, lane_pick(stay[c, h : h + 1], lo), got[c])
        for c in range(4):
            values[c, at] = got[c]
        return carry

    loads["slot"].wait()
    lax.fori_loop(0, 9, first_pick, 0)

    loads["wall"].wait()
    wall = jnp.where(
        (lax.broadcasted_iota(jnp.int32, (depth_z, 128), 1) == 0)
        | (lax.broadcasted_iota(jnp.int32, (depth_z, 128), 1) == 127),
        1,
        wall_ref[pl.ds(pl.multiple_of(me_z * depth_z, depth_z), depth_z)],
    )
    solid[PAD : PAD + depth_z] = wall
    lane = lax.broadcasted_iota(jnp.int32, (1, 128), 1)
    ends = (lane == 0) | (lane == 127)
    below = lax.rem(me_z * depth_z + rows_z - 1, rows_z)
    above = lax.rem(me_z * depth_z + depth_z, rows_z)
    solid[PAD - 1 : PAD] = jnp.where(ends, 1, wall_ref[pl.ds(below, 1)])
    solid[PAD + depth_z : PAD + depth_z + 1] = jnp.where(ends, 1, wall_ref[pl.ds(above, 1)])

    loads["weight"].wait()
    loads["cell"].wait()
    loads["rates"].wait()
    loads["pops"].wait()
    for copy in migrations:
        copy.wait()

    def second_pick(j, carry):
        at = pl.ds(j * 8 if isinstance(j, int) else pl.multiple_of(j * 8, 8), 8)
        slots = slot_ref[at]
        hi, lo = slots >> 7, slots & 127
        got = [values[c, at] for c in range(4)]
        for d in range(4):
            hit = hi == 16 + d
            for c in range(4):
                got[c] = jnp.where(hit, lane_pick(arrive[d, c : c + 1], lo), got[c])
        scale = weight_ref[at] * got[3]
        for c in range(3):
            values[c, at] = scale * got[c]
        values[3, at] = scale
        return carry

    def outer_pick(n, carry):
        return second_pick(jnp.where(n >= 4, n + 1, n), carry)

    lax.fori_loop(0, 8, outer_pick, 0)

    def bucket(step_x, step_z):
        at = ((step_x + 1) * 3 + step_z + 1) * 8
        cells = cell_ref[at : at + 8]
        return [values[c, at : at + 8] for c in range(4)], cells

    exchanges = []
    for s, step in enumerate(STEP):
        total = None
        for step_x in (-1, 0, 1):
            got, cells = bucket(step_x, step)
            rows = (cells >> 11) + 1 if step_x == 0 else jnp.full_like(cells, 0 if step_x < 0 else 5)
            part = spread(got, rows, cells & 127, 8)
            total = part if total is None else total + part
        edge_out[s] = total.reshape(4, 8, 128)
        exchanges.append(send(edge_out.at[s], edge_in.at[s], (0, step)))
        for sx, step_x in enumerate(STEP):
            at = s * 2 + sx
            row = 5 if step_x == 1 else 0
            for c in range(4):
                corner_out[at, c : c + 1] = total[c * 8 + row : c * 8 + row + 1]
            exchanges.append(send(corner_out.at[at], corner_in.at[at], (step_x, step)))
    for s, step in enumerate(STEP):
        got, cells = bucket(step, 0)
        plane_out[s] = spread(got, (cells >> 7) & 15, cells & 127, 16).reshape(4, 16, 128)
        exchanges.append(send(plane_out.at[s], plane_in.at[s], (step, 0)))
    second_pick(4, 0)
    got, cells = bucket(0, 0)
    force[...] = spread(got, cells >> 7, cells & 127, 64).reshape(4, 4, 16, 128)
    for copy in exchanges:
        copy.wait()
    for s in range(2):
        x = 0 if s == 0 else 3
        for c in range(4):
            force[c, x] = force[c, x] + plane_in[s, c]
    for s in range(2):
        z = 0 if s == 0 else 15
        for c in range(4):
            for x in range(4):
                row = edge_in[s, c, x + 1 : x + 2]
                if x == 0:
                    row = row + corner_in[s * 2, c : c + 1]
                if x == 3:
                    row = row + corner_in[s * 2 + 1, c : c + 1]
                force[c, x, z : z + 1] = force[c, x, z : z + 1] + row

    rates = [rates_ref[k] for k in range(19)]
    halos = []
    for x in (3, 0, 1, 2):
        done = collide(
            [pops_ref[q, x] for q in range(19)],
            [force[c, x] for c in range(4)],
            rates,
            range(19),
        )
        for q in range(19):
            coll[q, 1 + x, PAD : PAD + 16] = done[q]
        for s in range(2):
            z = 15 if s == 0 else 0
            for n, q in enumerate(ALONG_Z[s]):
                halo_z_out[s, n, x : x + 1] = done[q][z : z + 1]
        if x in (3, 0):
            s = 0 if x == 3 else 1
            for n, q in enumerate(ALONG_X[s]):
                halo_x_out[s, n] = done[q]
            for sz in range(2):
                q = VELOCITIES.index((STEP[s], 0, STEP[sz]))
                z = 15 if sz == 0 else 0
                at = sz * 2 + s
                halo_c_out[at, 0:1] = done[q][z : z + 1]
                halos.append(send(halo_c_out.at[at], halo_c_in.at[at], (STEP[s], STEP[sz])))
            halos.append(send(halo_x_out.at[s], halo_x_in.at[s], (STEP[s], 0)))
    for s in range(2):
        halos.append(send(halo_z_out.at[s], halo_z_in.at[s], (0, STEP[s])))
    def stream(late):
        for q in range(19):
            step_x, step_y, step_z = VELOCITIES[q]
            for half in range(2):
                chosen = [
                    x
                    for x in range(4)
                    if late
                    == (
                        (step_x, x) in ((1, 0), (-1, 3)) or (step_z, half) in ((1, 0), (-1, 1))
                    )
                ]
                if not chosen:
                    continue
                at = PAD + 8 * half
                blocked = solid[at - step_z : at - step_z + 8]
                if step_y:
                    blocked = pltpu.roll(blocked, step_y % 128, 1)
                for x in chosen:
                    moved = coll[q, 1 + x - step_x, at - step_z : at - step_z + 8]
                    if step_y:
                        moved = pltpu.roll(moved, step_y % 128, 1)
                    out_ref[q, x, 8 * half : 8 * half + 8] = jnp.where(
                        blocked > 0, coll[OPPOSITE[q], 1 + x, at : at + 8], moved
                    )

    stream(False)
    for copy in halos:
        copy.wait()
    for s in range(2):
        for n, q in enumerate(ALONG_X[s]):
            coll[q, 0 if s == 0 else 5, PAD : PAD + 16] = halo_x_in[s, n]
        z = PAD - 1 if s == 0 else PAD + 16
        for n, q in enumerate(ALONG_Z[s]):
            for x in range(4):
                coll[q, 1 + x, z : z + 1] = halo_z_in[s, n, x : x + 1]
        for sx in range(2):
            q = VELOCITIES.index((STEP[sx], 0, STEP[s]))
            coll[q, 0 if sx == 0 else 5, z : z + 1] = halo_c_in[s * 2 + sx, 0:1]

    stream(True)


def solution(mesh):
    devices_x, devices_z = mesh.shape["gx"], mesh.shape["gz"]

    def body(pops, rates, wall, particles, lists, slot, cell, weight):
        vmem = pl.BlockSpec(memory_space=pltpu.VMEM)
        hbm = pl.BlockSpec(memory_space=pltpu.HBM)
        f32 = jnp.float32
        return pl.pallas_call(
            lambda *refs: kernel(devices_x, devices_z, *refs),
            out_shape=pltpu.VMEM(pops.shape, f32),
            in_specs=[hbm] * 8,
            out_specs=vmem,
            scratch_shapes=[
                pltpu.VMEM(pops.shape, f32),
                pltpu.SMEM(rates.shape, f32),
                pltpu.VMEM(wall.shape, jnp.int32),
                pltpu.VMEM((64, 128), f32),
                pltpu.VMEM((4, 128), jnp.int32),
                pltpu.VMEM((72, 128), jnp.int32),
                pltpu.VMEM((72, 128), jnp.int32),
                pltpu.VMEM((72, 128), f32),
                pltpu.SemaphoreType.DMA((8,)),
                pltpu.VMEM((4, 16, 128), f32),
                pltpu.VMEM((4, 8, 128), f32),
                pltpu.VMEM((4, 8, 128), f32),
                pltpu.VMEM((4, 72, 128), f32),
                pltpu.VMEM((4, 4, 16, 128), f32),
                pltpu.VMEM((2, 4, 16, 128), f32),
                pltpu.VMEM((2, 4, 16, 128), f32),
                pltpu.VMEM((2, 4, 8, 128), f32),
                pltpu.VMEM((2, 4, 8, 128), f32),
                pltpu.VMEM((4, 4, 128), f32),
                pltpu.VMEM((4, 4, 128), f32),
                pltpu.VMEM((19, 6, 32, 128), f32),
                pltpu.VMEM((2, 5, 16, 128), f32),
                pltpu.VMEM((2, 5, 16, 128), f32),
                pltpu.VMEM((2, 5, 8, 128), f32),
                pltpu.VMEM((2, 5, 8, 128), f32),
                pltpu.VMEM((4, 8, 128), f32),
                pltpu.VMEM((4, 8, 128), f32),
                pltpu.VMEM((32, 128), jnp.int32),
                pltpu.SemaphoreType.DMA((20,)),
                pltpu.SemaphoreType.DMA((20,)),
            ],
            compiler_params=pltpu.CompilerParams(
                collective_id=0, has_side_effects=True, vmem_limit_bytes=56000 * 1024
            ),
        )(
            pops,
            rates,
            wall,
            particles.reshape(64, 128),
            lists.reshape(4, 128),
            slot.reshape(72, 128),
            cell.reshape(72, 128),
            weight.reshape(72, 128),
        )

    return jax.shard_map(
        body,
        mesh=mesh,
        in_specs=(
            P(None, "gx", "gz", None),
            P(),
            P(),
            P(None, "gx", "gz", None),
            P("gx", "gz", None, None),
            P("gx", "gz", None, None),
            P("gx", "gz", None, None),
            P("gx", "gz", None, None),
        ),
        out_specs=P(None, "gx", "gz", None),
        check_vma=False,
    )
```
